32 devices in a mesh: expert: 8 (over z, x), dp: 4 (over y, core).
Axes of the slice: x: 2, y: 2, z: 4, core: 2. Of those that a mesh axis runs over, the one named last changes fastest.
Arguments:
- tokens: bfloat16 [2048, 2048], P('expert'), may hold values from -6 to 6
- cotangent: bfloat16 [2048, 2048], P('expert'), may hold values from -6 to 6
- expert_route: int32 [2048, 1], P('expert'), may hold values from 0 to 7; in each aligned block of 256 rows (0 to 255, 256 to 511, ...) at most 64 rows name the same one
- w_gate: bfloat16 [8, 2048, 7168], P('expert', None, 'dp'), may hold values from -0.125 to 0.125
- w_up: bfloat16 [8, 2048, 7168], P('expert', None, 'dp'), may hold values from -0.125 to 0.125
- w_down: bfloat16 [8, 7168, 2048], P('expert', 'dp'), may hold values from -0.0625 to 0.0625
- sign_seeds: int32 [8], P('expert'), may hold values from 0 to 65535
Outputs:
- tangent_grad: bfloat16 [2048, 2048], P('expert')
- curvature: float32 [8, 7168], P('expert', 'dp')
The draws below stay inside these ranges and needn't reach their ends.
Inputs may be any that keep to these rules, and one draw needn't show every extreme that they name: `expert_route`: among the tokens of one index of expert no expert is named more than 64 times, and in some index one expert is named exactly 64 times; every expert is named by some token.
All inputs are finite; a program needn't handle non-finite values.
Results may differ from the reference program's by a relative error of at most 0.005.
Values may be sent and summed in bfloat16 or wider, within the bound.
A program may use at most 128 MiB of HBM per device.

```python
import math
import jax
import jax.numpy as jnp
import numpy as np
from jax import lax

D = 2048
FF = 7168
TOK_DEV = 256
EXPERTS = 8
CAP = 64
TOKENS = 2048
N_EXPERT = 8


def set_ends(result, stream_key, smallest, largest):
    shape = result.shape
    spot = [jax.random.randint(jax.random.fold_in(stream_key, axis), (), 0, shape[axis]) for axis in range(len(shape))]
    result = result.at[tuple(spot)].set(smallest)
    longest = shape.index(max(shape))
    spot[longest] = (spot[longest] + 1) % shape[longest]
    return result.at[tuple(spot)].set(largest)


def levels(rng, dims, split, least, largest):
    def one(dim, blocks):
        draws = jax.random.uniform(jax.random.fold_in(jax.random.fold_in(rng, 6), dim), (blocks,), jnp.float32, least / len(split), largest / len(split))
        return jnp.repeat(jnp.exp(draws), dims[dim] // blocks).reshape((-1,) + (1,) * (len(dims) - dim - 1))

    level = one(*split[0])
    for cut in split[1:]:
        level = level * one(*cut)
    return level


def assign_block(rng, own, number, rows, count, top, most, slope):
    ranking = jax.random.permutation(rng, count)
    heavy_load, ordinary = shares(count, rows * top, most, slope, True), shares(count, rows * top, most, slope, False)
    places = jnp.arange(count)

    def named(sizes, rotation):
        used = int((sizes > 0).sum())
        fixed = max(1, used // 4)
        passed = fixed + (places - fixed + rotation * (used - fixed)) % max(1, count - fixed)
        return jnp.zeros((count,), jnp.int32).at[ranking[jnp.where(places < fixed, places, passed)]].set(jnp.asarray(sizes, jnp.int32))

    sizes = jnp.where(number % 4 == 0, named(heavy_load, number // 4), named(ordinary, number - number // 4 - 1))
    mixed = jax.random.permutation(jax.random.fold_in(own, 3), count)
    source_of, sink = mixed[0:count // 2 * 2:2], mixed[1:count // 2 * 2:2]
    room = jnp.minimum(sizes[source_of] - 1, most - sizes[sink]) // 2
    room = jnp.where((source_of == ranking[0]) | (sink == ranking[0]) | (sizes[sink] == 0), 0, jnp.maximum(room, 0))
    passed = jax.random.randint(jax.random.fold_in(own, 4), (count // 2,), 0, 1 << 20) % (room + 1)
    sizes = sizes.at[source_of].add(-passed).at[sink].add(passed)
    labels = jnp.searchsorted(jnp.cumsum(sizes), jnp.arange(rows * top), side="right").astype(jnp.int32)
    listing = labels.reshape(top, rows).T
    listing = listing[jax.random.permutation(jax.random.fold_in(own, 1), rows)]
    rotation = jax.random.randint(jax.random.fold_in(own, 2), (rows, 1), 0, top)
    return jnp.take_along_axis(listing, (jnp.arange(top)[None, :] + rotation) % top, axis=1)


def shares(count, total, reach, lean, full):
    loads = [(1 << 20) // math.isqrt(standing ** lean) + 1 for standing in range(1, count + 1)]
    largest = reach if full else min(reach, max(-(-total // count), total * loads[0] // sum(loads)))
    least = 1 if total - largest >= count - 1 else 0
    given, rest = [largest] + [least] * (count - 1), total - largest - least * (count - 1)
    while rest > 0:
        free = [i for i in range(1, count) if given[i] < largest] or [i for i in range(1, count) if given[i] < reach]
        whole, budget = sum([loads[i] for i in free]), rest
        for i in free:
            more = min(reach - given[i], max(1, budget * loads[i] // whole), rest)
            given[i] = given[i] + more
            rest = rest - more
    return np.array(given)


def centred(own_key, dims, width, bound, split=(), kind=jnp.bfloat16):
    values = jax.random.normal(own_key, dims, jnp.float32) * width
    if len(split) > 0:
        values = levels(own_key, dims, split, -0.22, 0.18) * values
    return jnp.clip(values, min=-bound, max=bound).astype(kind)


def setup_inputs(seed: int = 0) -> dict:
    arg_keys = jax.random.split(jax.random.key(seed), 8)
    tokens = centred(arg_keys[0], (TOKENS, D), 1.0, 6.0, ((0, 8),))
    cotangent = centred(arg_keys[1], (TOKENS, D), 1.0, 6.0, ((0, 8),))
    expert_route_keys = jax.random.split(jax.random.fold_in(arg_keys[2], 1), TOKENS // TOK_DEV)
    expert_route_turns = jax.random.permutation(jax.random.fold_in(arg_keys[2], 3), TOKENS // TOK_DEV)
    expert_route = jax.vmap(lambda own, number: assign_block(jax.random.fold_in(arg_keys[2], 2), own, number, TOK_DEV, EXPERTS, 1, CAP, 2))(expert_route_keys, expert_route_turns).reshape((TOKENS, 1))
    w_gate = centred(arg_keys[3], (EXPERTS, D, FF), D ** -0.5, 0.125, ((0, 8), (2, 4)))
    w_up = centred(arg_keys[4], (EXPERTS, D, FF), D ** -0.5, 0.125, ((0, 8), (2, 4)))
    w_down = centred(arg_keys[5], (EXPERTS, FF, D), FF ** -0.5, 0.0625, ((0, 8), (1, 4)))
    sign_seeds = set_ends(jax.random.randint(arg_keys[6], (EXPERTS,), 0, 65536), jax.random.fold_in(arg_keys[6], 1), 0, 65535).astype(jnp.int32)
    return dict(tokens=tokens, cotangent=cotangent, expert_route=expert_route, w_gate=w_gate, w_up=w_up, w_down=w_down, sign_seeds=sign_seeds)


def mix_bits(row_index, col_index, seed_value):
    mixed = row_index * jnp.int32(73856093) + col_index * jnp.int32(19349663) + seed_value * jnp.int32(83492791)
    mixed = mixed ^ mixed >> 15
    mixed = mixed * jnp.int32(735632791)
    mixed = mixed ^ mixed >> 13
    mixed = mixed * jnp.int32(1274126177)
    mixed = mixed ^ mixed >> 16
    return mixed >> 5 & 1

def sign_table(row_index, col_index, seed_value, model_width):
    bits = mix_bits(row_index, col_index, seed_value)
    scale = jnp.asarray(1.0 / math.sqrt(model_width), jnp.bfloat16)
    return jnp.where(bits == 1, scale, -scale)

def silu_slopes(pre_act):
    sigmoid_pre = jax.nn.sigmoid(pre_act)
    slope_one = sigmoid_pre * (1.0 + pre_act * (1.0 - sigmoid_pre))
    slope_two = sigmoid_pre * (1.0 - sigmoid_pre) * (2.0 + pre_act * (1.0 - 2.0 * sigmoid_pre))
    return (slope_one, slope_two)

def expert_rows(rows_x, rows_cot, gate_mat, up_mat, down_mat, sign_values):
    contract = (((1,), (1,)), ((), ()))
    gate_pre = jnp.dot(rows_x, gate_mat, preferred_element_type=jnp.float32)
    up_pre = jnp.dot(rows_x, up_mat, preferred_element_type=jnp.float32)
    gate_tangent = jnp.dot(rows_x, sign_values, preferred_element_type=jnp.float32)
    hidden_grad = lax.dot_general(rows_cot, down_mat, contract, preferred_element_type=jnp.float32)
    slope_one, slope_two = silu_slopes(gate_pre)
    grad_gate = (hidden_grad * up_pre * slope_one).astype(jnp.bfloat16)
    tangent_gate = hidden_grad * up_pre * slope_two * gate_tangent
    tangent_up = (hidden_grad * slope_one * gate_tangent).astype(jnp.bfloat16)
    curvature = lax.optimization_barrier(jnp.sum(gate_tangent * tangent_gate, axis=0))
    tangent_grads = lax.dot_general(tangent_gate.astype(jnp.bfloat16), gate_mat, contract, preferred_element_type=jnp.float32)
    tangent_grads = tangent_grads + lax.dot_general(tangent_up, up_mat, contract, preferred_element_type=jnp.float32)
    tangent_grads = tangent_grads + lax.dot_general(grad_gate, sign_values, contract, preferred_element_type=jnp.float32)
    return (tangent_grads, curvature)

def reference(tokens, cotangent, expert_route, w_gate, w_up, w_down, sign_seeds):
    route_flat = expert_route[:, 0].astype(jnp.int32)
    expert_ids = jnp.arange(EXPERTS, dtype=jnp.int32)
    counts = lax.optimization_barrier(jnp.sum((route_flat[:, None] == expert_ids[None, :]).astype(jnp.int32), axis=0))
    starts = (jnp.cumsum(counts) - counts).astype(jnp.int32)
    most_rows = CAP * N_EXPERT
    sorted_tokens = jnp.argsort(route_flat, stable=True).astype(jnp.int32)
    padded_tokens = jnp.concatenate([sorted_tokens, jnp.zeros((most_rows,), jnp.int32)])
    row_index = jnp.arange(D, dtype=jnp.int32)[:, None]
    col_index = jnp.arange(FF, dtype=jnp.int32)[None, :]

    def one_expert(accumulated, expert_index):
        picked = lax.dynamic_slice_in_dim(padded_tokens, starts[expert_index].astype(jnp.int32), most_rows)
        live_rows = jnp.arange(most_rows, dtype=jnp.int32) < counts[expert_index]
        rows_x = jnp.where(live_rows[:, None], tokens[picked], jnp.zeros((), tokens.dtype))
        rows_cot = jnp.where(live_rows[:, None], cotangent[picked], jnp.zeros((), cotangent.dtype))
        sign_values = sign_table(row_index, col_index, sign_seeds[expert_index], D)
        tangent_grads, curvature = expert_rows(rows_x, rows_cot, w_gate[expert_index], w_up[expert_index], w_down[expert_index], sign_values)
        masked = jnp.where(live_rows[:, None], tangent_grads, jnp.zeros((), jnp.float32))
        accumulated = accumulated.at[picked].add(masked)
        return (accumulated, curvature)
    start_total = jnp.zeros((TOKENS, D), jnp.float32)
    total, curvature = lax.scan(one_expert, start_total, expert_ids)
    return (total.astype(jnp.bfloat16), curvature)
```

```python
import functools
import math

import jax
import jax.numpy as jnp
import ml_dtypes
from jax import lax
from jax.experimental import pallas as pl
from jax.experimental.pallas import tpu as pltpu
from jax.sharding import PartitionSpec as P

MESH = pl.DeviceIdType.MESH
CORES = 2
LAG = 2
NT = (((1,), (1,)), ((), ()))


def loop(low, high, fn):
    def step(index, carry):
        fn(index)
        return carry

    lax.fori_loop(low, high, step, 0)


def kernel(
    cfg,
    route_col, route_row, seed, tok, cot, wg_hbm, wu_hbm, wd_hbm,
    out_hbm, curv,
    wg, wu, wd, sign, base, disp, disp_t, tq, sb, xb, pre, lin, dpre, tgate, tup, ggate,
    ksend, krecv, ysend, yrecv, fin, ret, ob,
    w_sem, t_sem, out_sem, a_send, a_recv, y_send, y_recv, c_send, c_recv,
    k_send, k_recv, p_send, p_recv, b_send, b_recv, oy_send, oy_recv, oc_send, oc_recv,
):
    experts, dps, toks, width, hidden, slots, fc, qw, ch = cfg
    ys = dps // CORES
    rounds = qw // ch
    chunks = hidden // fc
    rows = experts * slots
    me = lax.axis_index("expert")
    mine = lax.axis_index("dp")
    core = lax.rem(mine, CORES)
    y = lax.div(mine, CORES)
    sibling = (me, y * CORES + 1 - core)

    def expert_at(k):
        return lax.rem(me + k, experts)

    def expert_from(k):
        return lax.rem(me - k + experts, experts)

    def y_at(dy):
        return lax.rem(y + dy, ys)

    def y_from(dy):
        return lax.rem(y - dy + ys, ys)

    def y_peer(dy):
        return (me, y_at(dy) * CORES + core)

    def row_block(e):
        return pl.ds(pl.multiple_of(e * slots, slots), slots)

    def quarter(d):
        return pl.ds(pl.multiple_of(d * qw, qw), qw)

    def remote(src, dst, s, r, dev):
        return pltpu.make_async_remote_copy(
            src_ref=src, dst_ref=dst, send_sem=s, recv_sem=r, device_id=dev, device_id_type=MESH
        )

    tok_loads = [
        pltpu.make_async_copy(ref.at[:, quarter(mine)], tq.at[i], t_sem.at[i])
        for i, ref in enumerate((tok, cot))
    ]
    for load in tok_loads:
        load.start()
    w_loads = [
        pltpu.make_async_copy(src.at[0], dst, w_sem.at[i])
        for i, (src, dst) in enumerate(((wg_hbm, wg), (wu_hbm, wu), (wd_hbm, wd)))
    ]
    for load in w_loads:
        load.start()

    barrier = pltpu.get_barrier_semaphore()
    loop(1, experts, lambda k: pl.semaphore_signal(
        barrier, inc=1, device_id=(expert_at(k), mine), device_id_type=MESH))
    loop(1, ys, lambda dy: pl.semaphore_signal(
        barrier, inc=1, device_id=y_peer(dy), device_id_type=MESH))
    pl.semaphore_signal(barrier, inc=1, device_id=sibling, device_id_type=MESH)

    def iota(shape, dim):
        return lax.broadcasted_iota(jnp.int32, shape, dim)

    def ones_where(cond):
        return jnp.where(cond, 1.0, 0.0).astype(jnp.float32)

    pad = max(16, experts)
    hot = ones_where(iota((pad, toks), 0) == route_row[...])
    upper = ones_where(iota((toks, toks), 0) <= iota((toks, toks), 1)).astype(jnp.bfloat16)
    seen = jnp.dot(hot.astype(jnp.bfloat16), upper, preferred_element_type=jnp.float32)
    place = jnp.sum(seen * hot, axis=0, keepdims=True) - 1.0
    target = route_row[...] * slots + place.astype(jnp.int32)
    disp[...] = ones_where(iota((rows, toks), 0) == target).astype(jnp.bfloat16)

    def a_copy(i, k):
        e = expert_at(k)
        return remote(sb.at[i, row_block(e), :], xb.at[i, row_block(me), quarter(mine)],
                      a_send.at[i, k], a_recv.at[i, k], (e, mine))

    def a_landed(i, k):
        spot = xb.at[i, row_block(expert_from(k)), quarter(mine)]
        return remote(spot, spot, a_send.at[i, k], a_recv.at[i, k], (expert_from(k), mine))

    def y_copy(i, dy, k):
        spot = xb.at[i, row_block(expert_from(k)), quarter(mine)]
        return remote(spot, spot, y_send.at[i, dy, k], y_recv.at[i, dy, k], y_peer(dy))

    def c_copy(i, dy, k):
        d = y_from(dy) * CORES + core
        spot = xb.at[i, row_block(expert_from(k)), quarter(d)]
        return remote(spot, spot, c_send.at[i, dy, k], c_recv.at[i, dy, k], sibling)

    def y_landed(i, dy, k):
        d = y_from(dy) * CORES + core
        spot = xb.at[i, row_block(expert_from(k)), quarter(d)]
        return remote(spot, spot, y_send.at[i, dy, k], y_recv.at[i, dy, k], y_peer(dy))

    def c_landed(i, dy, k):
        d = y_from(dy) * CORES + 1 - core
        spot = xb.at[i, row_block(expert_from(k)), quarter(d)]
        return remote(spot, spot, c_send.at[i, dy, k], c_recv.at[i, dy, k], sibling)

    def dispatch(i):
        tok_loads[i].wait()
        sb[i] = jnp.dot(disp[...], tq[i], preferred_element_type=jnp.float32).astype(jnp.bfloat16)

    def keep_own(i):
        xb[i, row_block(me), quarter(mine)] = sb[i, row_block(me), :]

    def forward(i, k):
        @pl.when(k > 0)
        def _():
            a_landed(i, k).wait_recv()

        loop(1, ys, lambda dy: y_copy(i, dy, k).start())
        c_copy(i, 0, k).start()

    def second_hop(i, k):
        def one(dy):
            y_landed(i, dy, k).wait_recv()
            c_copy(i, dy, k).start()

        loop(1, ys, one)

    def all_landed(i):
        loop(0, experts, lambda k: loop(0, ys, lambda dy: c_landed(i, dy, k).wait_recv()))

    dispatch(0)
    keep_own(0)
    pl.semaphore_wait(barrier, experts - 1 + ys)
    loop(1, experts, lambda k: a_copy(0, k).start())
    dispatch(1)
    keep_own(1)

    hot_t = ones_where(iota((toks, 128), 1) == route_col[...])
    lower = ones_where(iota((toks, toks), 0) >= iota((toks, toks), 1)).astype(jnp.bfloat16)
    seen_t = jnp.dot(lower, hot_t.astype(jnp.bfloat16), preferred_element_type=jnp.float32)
    place_t = jnp.sum(seen_t * hot_t, axis=1, keepdims=True) - 1.0
    target_t = route_col[...] * slots + place_t.astype(jnp.int32)
    disp_t[...] = ones_where(iota((toks, rows), 1) == target_t).astype(jnp.bfloat16)

    scale = float(ml_dtypes.bfloat16(1.0 / math.sqrt(width)))
    band = 16
    base[...] = (
        iota((band, hidden), 0) * 73856093
        + (iota((band, hidden), 1) + mine * hidden) * 19349663
        + seed[0] * 83492791
    )

    def sign_rows(row0):
        m = base[...] + row0 * 73856093
        m = m ^ (m >> 15)
        m = m * 735632791
        m = m ^ (m >> 13)
        m = m * 1274126177
        m = m ^ (m >> 16)
        sign[pl.ds(pl.multiple_of(row0, band), band), :] = jnp.where(
            (m & 32) != 0, scale, -scale).astype(jnp.bfloat16)

    part = width // experts

    def first_steps(k):
        forward(0, k)

        @pl.when(k > 0)
        def _():
            a_copy(1, k).start()

        @pl.when(k >= LAG)
        def _():
            second_hop(0, k - LAG)

        loop(0, part // band, lambda j: sign_rows(k * part + j * band))

    loop(0, experts, first_steps)
    loop(experts - LAG, experts, lambda k: second_hop(0, k))
    w_loads[0].wait()
    w_loads[1].wait()
    all_landed(0)

    def cols(c):
        return pl.ds(pl.multiple_of(c * fc, fc), fc)

    def first_dots(c):
        forward(1, c)

        @pl.when(c >= LAG)
        def _():
            second_hop(1, c - LAG)

        x = xb[0]
        pre[c] = jnp.dot(x, wg[:, cols(c)], preferred_element_type=jnp.float32)
        lin[c] = jnp.dot(x, wu[:, cols(c)], preferred_element_type=jnp.float32)
        dpre[c] = jnp.dot(x, sign[:, cols(c)], preferred_element_type=jnp.float32)

    early = min(chunks, experts)
    loop(0, early, first_dots)
    loop(early, experts, lambda k: forward(1, k))
    loop(early - LAG, experts, lambda k: second_hop(1, k))
    w_loads[2].wait()
    all_landed(1)

    def gates(c):
        hgrad = lax.dot_general(xb[1], wd[cols(c), :], NT, preferred_element_type=jnp.float32)
        p, up, tangent = pre[c], lin[c], dpre[c]
        sig = jax.nn.sigmoid(p)
        slope = sig * (1.0 + p * (1.0 - sig))
        bend = sig * (1.0 - sig) * (2.0 + p * (1.0 - 2.0 * sig))
        both = hgrad * up
        tg = both * bend * tangent
        ggate[:, cols(c)] = (both * slope).astype(jnp.bfloat16)
        tup[:, cols(c)] = (hgrad * slope * tangent).astype(jnp.bfloat16)
        tgate[:, cols(c)] = tg.astype(jnp.bfloat16)
        curv[:, cols(c)] = jnp.sum(tangent * tg, axis=0, keepdims=True)

    loop(0, chunks, gates)

    def out_chunk(d, r):
        at = pl.ds(pl.multiple_of(d * qw + r * ch, ch), ch)
        total = lax.dot_general(tgate[...], wg[at, :], NT, preferred_element_type=jnp.float32)
        total += lax.dot_general(tup[...], wu[at, :], NT, preferred_element_type=jnp.float32)
        total += lax.dot_general(ggate[...], sign[at, :], NT, preferred_element_type=jnp.float32)
        return total

    def k_copy(dy, r):
        return remote(ksend.at[dy, r], krecv.at[dy, r], k_send.at[dy, r], k_recv.at[dy, r], sibling)

    def p_copy(dy, r):
        return remote(ysend.at[dy, r], yrecv.at[dy, r], p_send.at[dy, r], p_recv.at[dy, r], y_peer(dy))

    def b_copy(r, k):
        e = expert_at(k)
        return remote(fin.at[r, row_block(e), :], ret.at[r, row_block(me), :],
                      b_send.at[r, k], b_recv.at[r, k], (e, mine))

    def b_landed(r, k):
        spot = ret.at[r, row_block(expert_from(k)), :]
        return remote(spot, spot, b_send.at[r, k], b_recv.at[r, k], (expert_from(k), mine))

    def pair_sum(dy, r):
        ksend[dy, r] = out_chunk(y_at(dy) * CORES + 1 - core, r).astype(jnp.bfloat16)
        k_copy(dy, r).start()
        own = out_chunk(y_at(dy) * CORES + core, r)
        k_copy(dy, r).wait_recv()
        return own + krecv[dy, r].astype(jnp.float32)

    def far(step):
        dy, r = 1 + lax.div(step, rounds), lax.rem(step, rounds)
        ysend[dy, r] = pair_sum(dy, r).astype(jnp.bfloat16)
        p_copy(dy, r).start()

    def near(r):
        total = pair_sum(0, r)
        for dy in range(1, ys):
            p_copy(dy, r).wait_recv()
            total += yrecv[dy, r].astype(jnp.float32)
        fin[r] = total.astype(jnp.bfloat16)
        loop(1, experts, lambda k: b_copy(r, k).start())
        ret[r, row_block(me), :] = fin[r, row_block(me), :]

    loop(0, (ys - 1) * rounds, far)
    loop(0, rounds, near)

    def o_spot(d, r):
        return ob.at[:, pl.ds(pl.multiple_of(d * qw + r * ch, ch), ch)]

    def oy_copy(dy, r):
        spot = o_spot(mine, r)
        return remote(spot, spot, oy_send.at[dy, r], oy_recv.at[dy, r], y_peer(dy))

    def oy_landed(dy, r):
        spot = o_spot(y_from(dy) * CORES + core, r)
        return remote(spot, spot, oy_send.at[dy, r], oy_recv.at[dy, r], y_peer(dy))

    def oc_copy(dy, r):
        spot = o_spot(y_from(dy) * CORES + core, r)
        return remote(spot, spot, oc_send.at[dy, r], oc_recv.at[dy, r], sibling)

    def oc_landed(dy, r):
        spot = o_spot(y_from(dy) * CORES + 1 - core, r)
        return remote(spot, spot, oc_send.at[dy, r], oc_recv.at[dy, r], sibling)

    def combine(r):
        loop(1, experts, lambda k: b_landed(r, k).wait_recv())
        ob[:, pl.ds(pl.multiple_of(mine * qw + r * ch, ch), ch)] = jnp.dot(
            disp_t[...], ret[r], preferred_element_type=jnp.float32).astype(jnp.bfloat16)
        loop(1, ys, lambda dy: oy_copy(dy, r).start())
        oc_copy(0, r).start()

    loop(0, rounds, combine)

    def out_hop(r):
        def one(dy):
            oy_landed(dy, r).wait_recv()
            oc_copy(dy, r).start()

        loop(1, ys, one)

    loop(0, rounds, out_hop)
    loop(0, rounds, lambda r: loop(0, ys, lambda dy: oc_landed(dy, r).wait_recv()))
    write = pltpu.make_async_copy(ob, out_hbm, out_sem)
    write.start()

    def drain(i):
        def one(k):
            @pl.when(k > 0)
            def _():
                a_copy(i, k).wait_send()

            loop(1, ys, lambda dy: y_copy(i, dy, k).wait_send())
            loop(0, ys, lambda dy: c_copy(i, dy, k).wait_send())

        loop(0, experts, one)

    loop(0, 2, drain)

    def drain_out(r):
        loop(0, ys, lambda dy: k_copy(dy, r).wait_send())
        loop(1, ys, lambda dy: p_copy(dy, r).wait_send())
        loop(1, experts, lambda k: b_copy(r, k).wait_send())
        loop(1, ys, lambda dy: oy_copy(dy, r).wait_send())
        loop(0, ys, lambda dy: oc_copy(dy, r).wait_send())

    loop(0, rounds, drain_out)
    write.wait()


def body(tokens, cotangent, expert_route, w_gate, w_up, w_down, sign_seeds):
    experts = lax.axis_size("expert")
    dps = lax.axis_size("dp")
    toks, width = tokens.shape
    hidden = w_gate.shape[2]
    slots = max(2, 2 * toks // experts)
    rows = experts * slots
    ys = dps // CORES
    qw = width // dps
    ch = min(256, qw)
    rounds = qw // ch
    fc = 256 if hidden % 256 == 0 else 128
    chunks = hidden // fc
    cfg = (experts, dps, toks, width, hidden, slots, fc, qw, ch)
    bf, f32 = jnp.bfloat16, jnp.float32
    vm, dma = pltpu.VMEM, pltpu.SemaphoreType.DMA
    anywhere = pl.BlockSpec(memory_space=pl.ANY)
    in_vmem = pl.BlockSpec(memory_space=pltpu.VMEM)
    return pl.pallas_call(
        functools.partial(kernel, cfg),
        out_shape=(
            jax.ShapeDtypeStruct((toks, width), bf),
            jax.ShapeDtypeStruct((1, hidden), f32),
        ),
        in_specs=[in_vmem, in_vmem, pl.BlockSpec(memory_space=pltpu.SMEM)] + [anywhere] * 5,
        out_specs=(anywhere, in_vmem),
        scratch_shapes=[
            vm((width, hidden), bf), vm((width, hidden), bf), vm((hidden, width), bf),
            vm((width, hidden), bf), vm((16, hidden), jnp.int32),
            vm((rows, toks), bf), vm((toks, rows), bf),
            vm((2, toks, qw), bf), vm((2, rows, qw), bf), vm((2, rows, width), bf),
            vm((chunks, rows, fc), f32), vm((chunks, rows, fc), f32), vm((chunks, rows, fc), f32),
            vm((rows, hidden), bf), vm((rows, hidden), bf), vm((rows, hidden), bf),
            vm((ys, rounds, rows, ch), bf), vm((ys, rounds, rows, ch), bf),
            vm((ys, rounds, rows, ch), bf), vm((ys, rounds, rows, ch), bf),
            vm((rounds, rows, ch), bf), vm((rounds, rows, ch), bf),
            vm((toks, width), bf),
            dma((3,)), dma((2,)), dma,
            dma((2, experts)), dma((2, experts)),
            dma((2, ys, experts)), dma((2, ys, experts)),
            dma((2, ys, experts)), dma((2, ys, experts)),
            dma((ys, rounds)), dma((ys, rounds)),
            dma((ys, rounds)), dma((ys, rounds)),
            dma((rounds, experts)), dma((rounds, experts)),
            dma((ys, rounds)), dma((ys, rounds)),
            dma((ys, rounds)), dma((ys, rounds)),
        ],
        compiler_params=pltpu.CompilerParams(
            collective_id=0, has_side_effects=True, vmem_limit_bytes=63 * 1024 * 1024
        ),
    )(
        expert_route, expert_route.reshape(1, toks), sign_seeds,
        tokens, cotangent, w_gate, w_up, w_down,
    )


def solution(mesh):
    in_specs = (
        P("expert", None),
        P("expert", None),
        P("expert", None),
        P("expert", None, "dp"),
        P("expert", None, "dp"),
        P("expert", "dp", None),
        P("expert"),
    )
    out_specs = (P("expert", None), P("expert", "dp"))
    return jax.shard_map(body, mesh=mesh, in_specs=in_specs, out_specs=out_specs, check_vma=False)
```

```python
import functools
import math

import jax
import jax.numpy as jnp
import ml_dtypes
from jax import lax
from jax.experimental import pallas as pl
from jax.experimental.pallas import tpu as pltpu
from jax.sharding import PartitionSpec as P

MESH = pl.DeviceIdType.MESH
CORES = 2
LAG = 2
NT = (((1,), (1,)), ((), ()))


def loop(low, high, fn):
    def step(index, carry):
        fn(index)
        return carry

    lax.fori_loop(low, high, step, 0)


def kernel(
    cfg,
    route_row, seed, tok, cot, wg_hbm, wu_hbm, wd_hbm,
    out_hbm, curv,
    w3, wd, base, disp, disp_t, tq, sb, xb, first, h3,
    ksend, krecv, own, ysend, yrecv, fin, ret, ob,
    w_sem, t_sem, out_sem, a_send, a_recv, y_send, y_recv, c_send, c_recv,
    k_send, k_recv, p_send, p_recv, b_send, b_recv, oy_send, oy_recv, oc_send, oc_recv,
):
    experts, dps, toks, width, hidden, slots, fc, qw, ch = cfg
    ys = dps // CORES
    rounds = qw // ch
    chunks = hidden // fc
    rows = experts * slots
    me = lax.axis_index("expert")
    mine = lax.axis_index("dp")
    core = lax.rem(mine, CORES)
    y = lax.div(mine, CORES)
    sibling = (me, y * CORES + 1 - core)

    def expert_at(k):
        return lax.rem(me + k, experts)

    def expert_from(k):
        return lax.rem(me - k + experts, experts)

    def y_at(dy):
        return lax.rem(y + dy, ys)

    def y_from(dy):
        return lax.rem(y - dy + ys, ys)

    def y_peer(dy):
        return (me, y_at(dy) * CORES + core)

    def row_block(e):
        return pl.ds(pl.multiple_of(e * slots, slots), slots)

    def quarter(d):
        return pl.ds(pl.multiple_of(d * qw, qw), qw)

    def remote(src, dst, s, r, dev):
        return pltpu.make_async_remote_copy(
            src_ref=src, dst_ref=dst, send_sem=s, recv_sem=r, device_id=dev, device_id_type=MESH
        )

    tok_loads = [
        pltpu.make_async_copy(ref.at[:, quarter(mine)], tq.at[i], t_sem.at[i])
        for i, ref in enumerate((tok, cot))
    ]
    for load in tok_loads:
        load.start()
    w_loads = [
        pltpu.make_async_copy(
            src.at[0, :, pl.ds(c * fc, fc)], w3.at[:, pl.ds((3 * c + i) * fc, fc)], w_sem.at[i, c]
        )
        for c in range(chunks)
        for i, src in enumerate((wg_hbm, wu_hbm))
    ]
    w_loads.append(pltpu.make_async_copy(wd_hbm.at[0], wd, w_sem.at[2, 0]))
    for load in w_loads:
        load.start()

    barrier = pltpu.get_barrier_semaphore()
    loop(1, experts, lambda k: pl.semaphore_signal(
        barrier, inc=1, device_id=(expert_at(k), mine), device_id_type=MESH))
    loop(1, ys, lambda dy: pl.semaphore_signal(
        barrier, inc=1, device_id=y_peer(dy), device_id_type=MESH))
    pl.semaphore_signal(barrier, inc=1, device_id=sibling, device_id_type=MESH)

    def iota(shape, dim):
        return lax.broadcasted_iota(jnp.int32, shape, dim)

    def ones_where(cond):
        return jnp.where(cond, 1.0, 0.0).astype(jnp.float32)

    pad = max(16, experts)
    hot = ones_where(iota((pad, toks), 0) == route_row[...])
    upper = ones_where(iota((toks, toks), 0) <= iota((toks, toks), 1)).astype(jnp.bfloat16)
    seen = jnp.dot(hot.astype(jnp.bfloat16), upper, preferred_element_type=jnp.float32)
    place = jnp.sum(seen * hot, axis=0, keepdims=True) - 1.0
    target = route_row[...] * slots + place.astype(jnp.int32)
    spots = ones_where(iota((rows, toks), 0) == target)
    disp[...] = spots.astype(jnp.bfloat16)

    def a_copy(i, k):
        e = expert_at(k)
        return remote(sb.at[i, row_block(e), :], xb.at[i, row_block(me), quarter(mine)],
                      a_send.at[i, k], a_recv.at[i, k], (e, mine))

    def a_landed(i, k):
        spot = xb.at[i, row_block(expert_from(k)), quarter(mine)]
        return remote(spot, spot, a_send.at[i, k], a_recv.at[i, k], (expert_from(k), mine))

    def y_copy(i, dy, k):
        spot = xb.at[i, row_block(expert_from(k)), quarter(mine)]
        return remote(spot, spot, y_send.at[i, dy, k], y_recv.at[i, dy, k], y_peer(dy))

    def c_copy(i, dy, k):
        d = y_from(dy) * CORES + core
        spot = xb.at[i, row_block(expert_from(k)), quarter(d)]
        return remote(spot, spot, c_send.at[i, dy, k], c_recv.at[i, dy, k], sibling)

    def y_landed(i, dy, k):
        d = y_from(dy) * CORES + core
        spot = xb.at[i, row_block(expert_from(k)), quarter(d)]
        return remote(spot, spot, y_send.at[i, dy, k], y_recv.at[i, dy, k], y_peer(dy))

    def c_landed(i, dy, k):
        d = y_from(dy) * CORES + 1 - core
        spot = xb.at[i, row_block(expert_from(k)), quarter(d)]
        return remote(spot, spot, c_send.at[i, dy, k], c_recv.at[i, dy, k], sibling)

    def dispatch(i):
        tok_loads[i].wait()
        sb[i] = jnp.dot(disp[...], tq[i], preferred_element_type=jnp.float32).astype(jnp.bfloat16)

    def keep_own(i):
        xb[i, row_block(me), quarter(mine)] = sb[i, row_block(me), :]

    def forward(i, k):
        @pl.when(k > 0)
        def _():
            a_landed(i, k).wait_recv()

        loop(1, ys, lambda dy: y_copy(i, dy, k).start())
        c_copy(i, 0, k).start()

    def second_hop(i, k):
        def one(dy):
            y_landed(i, dy, k).wait_recv()
            c_copy(i, dy, k).start()

        loop(1, ys, one)

    def all_landed(i):
        loop(0, experts, lambda k: loop(0, ys, lambda dy: c_landed(i, dy, k).wait_recv()))

    dispatch(0)
    keep_own(0)
    pl.semaphore_wait(barrier, experts - 1 + ys)
    loop(1, experts, lambda k: a_copy(0, k).start())
    dispatch(1)
    keep_own(1)

    disp_t[...] = jnp.transpose(spots).astype(jnp.bfloat16)

    scale = float(ml_dtypes.bfloat16(1.0 / math.sqrt(width)))
    band = 16
    base[...] = (
        iota((band, hidden), 0) * 73856093
        + (iota((band, hidden), 1) + mine * hidden) * 19349663
        + seed[0] * 83492791
    )

    def sign_rows(row0):
        m = base[...] + row0 * 73856093
        m = m ^ (m >> 15)
        m = m * 735632791
        m = m ^ (m >> 13)
        m = m * 1274126177
        m = m ^ (m >> 16)
        signs = jnp.where((m & 32) != 0, scale, -scale).astype(jnp.bfloat16)
        for c in range(chunks):
            w3[pl.ds(pl.multiple_of(row0, band), band), pl.ds((3 * c + 2) * fc, fc)] = (
                signs[:, c * fc:(c + 1) * fc])

    part = width // experts

    def first_steps(k):
        forward(0, k)

        @pl.when(k > 0)
        def _():
            a_copy(1, k).start()

        @pl.when(k >= LAG)
        def _():
            second_hop(0, k - LAG)

        loop(0, part // band, lambda j: sign_rows(k * part + j * band))

    loop(0, experts, first_steps)
    loop(experts - LAG, experts, lambda k: second_hop(0, k))
    for load in w_loads[:-1]:
        load.wait()
    all_landed(0)

    def first_dots(c):
        forward(1, c)

        @pl.when(c >= LAG)
        def _():
            second_hop(1, c - LAG)

        first[c] = jnp.dot(
            xb[0], w3[:, pl.ds(pl.multiple_of(c * 3 * fc, 3 * fc), 3 * fc)],
            preferred_element_type=jnp.float32)

    early = min(chunks, experts)
    loop(0, early, first_dots)
    loop(early, experts, lambda k: forward(1, k))
    loop(early - LAG, experts, lambda k: second_hop(1, k))
    w_loads[-1].wait()
    all_landed(1)

    def gates(c, hgrad):
        lanes = [pl.ds(i * fc, fc) for i in range(3)]
        total = jnp.zeros((1, fc), jnp.float32)
        tall = 32
        for row in range(0, rows, tall):
            at = pl.ds(row, tall)
            hg = hgrad[row:row + tall]
            p, up, tangent = (first[c, at, lane] for lane in lanes)
            sig = jax.nn.sigmoid(p)
            slope = sig * (1.0 + p * (1.0 - sig))
            bend = sig * (1.0 - sig) * (2.0 + p * (1.0 - 2.0 * sig))
            both = hg * up
            tg = both * bend * tangent
            parts = (tg, hg * slope * tangent, both * slope)
            for i, value in enumerate(parts):
                h3[at, pl.ds((3 * c + i) * fc, fc)] = value.astype(jnp.bfloat16)
            total += jnp.sum(tangent * tg, axis=0, keepdims=True)
        curv[:, pl.ds(c * fc, fc)] = total

    for c in range(0, chunks, 2):
        n = min(2, chunks - c)
        hgrads = lax.dot_general(
            xb[1], wd[pl.ds(c * fc, n * fc), :], NT, preferred_element_type=jnp.float32)
        for i in range(n):
            gates(c + i, hgrads[:, i * fc:(i + 1) * fc])

    def block_at(d, r):
        index = (lax.div(d, CORES) * rounds + r) * CORES + lax.rem(d, CORES)
        return pl.multiple_of(index * ch, ch)

    def k_copy(dy, r):
        return remote(ksend.at[dy, r], krecv.at[dy, r], k_send.at[dy, r], k_recv.at[dy, r], sibling)

    def p_copy(dy, r):
        return remote(ysend.at[dy, r], yrecv.at[dy, r], p_send.at[dy, r], p_recv.at[dy, r], y_peer(dy))

    def b_copy(r, k):
        e = expert_at(k)
        return remote(fin.at[r, row_block(e), :], ret.at[r, row_block(me), :],
                      b_send.at[r, k], b_recv.at[r, k], (e, mine))

    def b_landed(r, k):
        spot = ret.at[r, row_block(expert_from(k)), :]
        return remote(spot, spot, b_send.at[r, k], b_recv.at[r, k], (expert_from(k), mine))

    def split(step):
        return lax.rem(1 + lax.div(step, rounds), ys), lax.rem(step, rounds)

    def multiply(step):
        dy, r = split(step)
        at = pl.ds(pl.multiple_of((y_at(dy) * rounds + r) * CORES * ch, CORES * ch), CORES * ch)
        pair = lax.dot_general(h3[...], w3[at, :], NT, preferred_element_type=jnp.float32)
        left, right = pair[:, :ch], pair[:, ch:]
        ksend[dy, r] = jnp.where(core == 0, right, left).astype(jnp.bfloat16)
        k_copy(dy, r).start()
        own[dy, r] = jnp.where(core == 0, left, right)

    def finish(step):
        dy, r = split(step)
        k_copy(dy, r).wait_recv()

        @pl.when(dy > 0)
        def _():
            ysend[dy, r] = (own[dy, r] + krecv[dy, r].astype(jnp.float32)).astype(jnp.bfloat16)
            p_copy(dy, r).start()

        @pl.when(dy == 0)
        def _():
            total = own[0, r] + krecv[0, r].astype(jnp.float32)
            for other in range(1, ys):
                p_copy(other, r).wait_recv()
                total += yrecv[other, r].astype(jnp.float32)
            fin[r] = total.astype(jnp.bfloat16)
            loop(1, experts, lambda k: b_copy(r, k).start())
            ret[r, row_block(me), :] = fin[r, row_block(me), :]

    def both_steps(step):
        multiply(step)

        @pl.when(step > 0)
        def _():
            finish(step - 1)

    loop(0, ys * rounds, both_steps)
    finish(ys * rounds - 1)

    def o_spot(d, r):
        return ob.at[:, pl.ds(block_at(d, r), ch)]

    def oy_copy(dy, r):
        spot = o_spot(mine, r)
        return remote(spot, spot, oy_send.at[dy, r], oy_recv.at[dy, r], y_peer(dy))

    def oy_landed(dy, r):
        spot = o_spot(y_from(dy) * CORES + core, r)
        return remote(spot, spot, oy_send.at[dy, r], oy_recv.at[dy, r], y_peer(dy))

    def oc_copy(dy, r):
        spot = o_spot(y_from(dy) * CORES + core, r)
        return remote(spot, spot, oc_send.at[dy, r], oc_recv.at[dy, r], sibling)

    def oc_landed(dy, r):
        spot = o_spot(y_from(dy) * CORES + 1 - core, r)
        return remote(spot, spot, oc_send.at[dy, r], oc_recv.at[dy, r], sibling)

    def combine(r):
        loop(1, experts, lambda k: b_landed(r, k).wait_recv())
        ob[:, pl.ds(block_at(mine, r), ch)] = jnp.dot(
            disp_t[...], ret[r], preferred_element_type=jnp.float32).astype(jnp.bfloat16)
        loop(1, ys, lambda dy: oy_copy(dy, r).start())
        oc_copy(0, r).start()

    loop(0, rounds, combine)

    def out_hop(r):
        def one(dy):
            oy_landed(dy, r).wait_recv()
            oc_copy(dy, r).start()

        loop(1, ys, one)

    loop(0, rounds, out_hop)
    loop(0, rounds, lambda r: loop(0, ys, lambda dy: oc_landed(dy, r).wait_recv()))
    write = pltpu.make_async_copy(ob, out_hbm, out_sem)
    write.start()

    def drain(i):
        def one(k):
            @pl.when(k > 0)
            def _():
                a_copy(i, k).wait_send()

            loop(1, ys, lambda dy: y_copy(i, dy, k).wait_send())
            loop(0, ys, lambda dy: c_copy(i, dy, k).wait_send())

        loop(0, experts, one)

    loop(0, 2, drain)

    def drain_out(r):
        loop(0, ys, lambda dy: k_copy(dy, r).wait_send())
        loop(1, ys, lambda dy: p_copy(dy, r).wait_send())
        loop(1, experts, lambda k: b_copy(r, k).wait_send())
        loop(1, ys, lambda dy: oy_copy(dy, r).wait_send())
        loop(0, ys, lambda dy: oc_copy(dy, r).wait_send())

    loop(0, rounds, drain_out)
    write.wait()


def body(tokens, cotangent, expert_route, w_gate, w_up, w_down, sign_seeds):
    experts = lax.axis_size("expert")
    dps = lax.axis_size("dp")
    toks, width = tokens.shape
    hidden = w_gate.shape[2]
    slots = max(2, 2 * toks // experts)
    rows = experts * slots
    ys = dps // CORES
    qw = width // dps
    ch = min(256, qw)
    rounds = qw // ch
    fc = 256 if hidden % 256 == 0 else 128
    chunks = hidden // fc
    cfg = (experts, dps, toks, width, hidden, slots, fc, qw, ch)
    bf, f32 = jnp.bfloat16, jnp.float32
    vm, dma = pltpu.VMEM, pltpu.SemaphoreType.DMA
    anywhere = pl.BlockSpec(memory_space=pl.ANY)
    in_vmem = pl.BlockSpec(memory_space=pltpu.VMEM)
    return pl.pallas_call(
        functools.partial(kernel, cfg),
        out_shape=(
            jax.ShapeDtypeStruct((toks, width), bf),
            jax.ShapeDtypeStruct((1, hidden), f32),
        ),
        in_specs=[in_vmem, pl.BlockSpec(memory_space=pltpu.SMEM)] + [anywhere] * 5,
        out_specs=(anywhere, in_vmem),
        scratch_shapes=[
            vm((width, 3 * hidden), bf), vm((hidden, width), bf), vm((16, hidden), jnp.int32),
            vm((rows, toks), bf), vm((toks, rows), bf),
            vm((2, toks, qw), bf), vm((2, rows, qw), bf), vm((2, rows, width), bf),
            vm((chunks, rows, 3 * fc), f32), vm((rows, 3 * hidden), bf),
            vm((ys, rounds, rows, ch), bf), vm((ys, rounds, rows, ch), bf),
            vm((ys, rounds, rows, ch), f32),
            vm((ys, rounds, rows, ch), bf), vm((ys, rounds, rows, ch), bf),
            vm((rounds, rows, ch), bf), vm((rounds, rows, ch), bf),
            vm((toks, width), bf),
            dma((3, chunks)), dma((2,)), dma,
            dma((2, experts)), dma((2, experts)),
            dma((2, ys, experts)), dma((2, ys, experts)),
            dma((2, ys, experts)), dma((2, ys, experts)),
            dma((ys, rounds)), dma((ys, rounds)),
            dma((ys, rounds)), dma((ys, rounds)),
            dma((rounds, experts)), dma((rounds, experts)),
            dma((ys, rounds)), dma((ys, rounds)),
            dma((ys, rounds)), dma((ys, rounds)),
        ],
        compiler_params=pltpu.CompilerParams(
            collective_id=0, has_side_effects=True, vmem_limit_bytes=63 * 1024 * 1024
        ),
    )(
        expert_route.reshape(1, toks), sign_seeds,
        tokens, cotangent, w_gate, w_up, w_down,
    )


def solution(mesh):
    in_specs = (
        P("expert", None),
        P("expert", None),
        P("expert", None),
        P("expert", None, "dp"),
        P("expert", None, "dp"),
        P("expert", "dp", None),
        P("expert"),
    )
    out_specs = (P("expert", None), P("expert", "dp"))
    return jax.shard_map(body, mesh=mesh, in_specs=in_specs, out_specs=out_specs, check_vma=False)
```

```python
import functools
import math

import jax
import jax.numpy as jnp
import ml_dtypes
from jax import lax
from jax.experimental import pallas as pl
from jax.experimental.pallas import tpu as pltpu
from jax.sharding import PartitionSpec as P

MESH = pl.DeviceIdType.MESH
CORES = 2
LAG = 2
WINDOW = 3
NT = (((1,), (1,)), ((), ()))


def loop(low, high, fn):
    def step(index, carry):
        fn(index)
        return carry

    lax.fori_loop(low, high, step, 0)


def kernel(
    cfg,
    route_row, seed, tok, cot, wg_hbm, wu_hbm, wd_hbm,
    out_hbm, curv,
    w3, wd, base, disp, disp_t, tq, sb, xb, first, h3,
    ksend, krecv, own, ysend, yrecv, fin, ret, ob,
    w_sem, t_sem, out_sem, a_send, a_recv, y_send, y_recv, c_send, c_recv,
    k_send, k_recv, p_send, p_recv, b_send, b_recv, oy_send, oy_recv, oc_send, oc_recv,
):
    experts, dps, toks, width, hidden, slots, fc, qw, ch = cfg
    ys = dps // CORES
    rounds = qw // ch
    chunks = hidden // fc
    rows = experts * slots
    window = min(WINDOW, experts - 1)
    me = lax.axis_index("expert")
    mine = lax.axis_index("dp")
    core = lax.rem(mine, CORES)
    y = lax.div(mine, CORES)
    sibling = (me, y * CORES + 1 - core)

    def expert_at(k):
        return lax.rem(me + k, experts)

    def expert_from(k):
        return lax.rem(me - k + experts, experts)

    def y_at(dy):
        return lax.rem(y + dy, ys)

    def y_from(dy):
        return lax.rem(y - dy + ys, ys)

    def y_peer(dy):
        return (me, y_at(dy) * CORES + core)

    def row_block(e):
        return pl.ds(pl.multiple_of(e * slots, slots), slots)

    def quarter(d):
        return pl.ds(pl.multiple_of(d * qw, qw), qw)

    def remote(src, dst, s, r, dev):
        return pltpu.make_async_remote_copy(
            src_ref=src, dst_ref=dst, send_sem=s, recv_sem=r, device_id=dev, device_id_type=MESH
        )

    tok_loads = [
        pltpu.make_async_copy(ref.at[:, quarter(mine)], tq.at[i], t_sem.at[i])
        for i, ref in enumerate((tok, cot))
    ]
    for load in tok_loads:
        load.start()
    w_loads = [
        pltpu.make_async_copy(
            src.at[0, :, pl.ds(c * fc, fc)], w3.at[:, pl.ds((3 * c + i) * fc, fc)], w_sem.at[i, c]
        )
        for c in range(chunks)
        for i, src in enumerate((wg_hbm, wu_hbm))
    ]
    w_loads.append(pltpu.make_async_copy(wd_hbm.at[0], wd, w_sem.at[2, 0]))
    for load in w_loads:
        load.start()

    barrier = pltpu.get_barrier_semaphore()
    loop(1, experts, lambda k: pl.semaphore_signal(
        barrier, inc=1, device_id=(expert_at(k), mine), device_id_type=MESH))
    loop(1, ys, lambda dy: pl.semaphore_signal(
        barrier, inc=1, device_id=y_peer(dy), device_id_type=MESH))
    pl.semaphore_signal(barrier, inc=1, device_id=sibling, device_id_type=MESH)

    def iota(shape, dim):
        return lax.broadcasted_iota(jnp.int32, shape, dim)

    def ones_where(cond):
        return jnp.where(cond, 1.0, 0.0).astype(jnp.float32)

    pad = max(16, experts)
    hot = ones_where(iota((pad, toks), 0) == route_row[...])
    upper = ones_where(iota((toks, toks), 0) <= iota((toks, toks), 1)).astype(jnp.bfloat16)
    seen = jnp.dot(hot.astype(jnp.bfloat16), upper, preferred_element_type=jnp.float32)
    place = jnp.sum(seen * hot, axis=0, keepdims=True) - 1.0
    target = route_row[...] * slots + place.astype(jnp.int32)
    spots = ones_where(iota((rows, toks), 0) == target)
    disp[...] = spots.astype(jnp.bfloat16)

    def a_copy(i, k):
        e = expert_at(k)
        return remote(sb.at[i, row_block(e), :], xb.at[i, row_block(me), quarter(mine)],
                      a_send.at[i, k], a_recv.at[i, k], (e, mine))

    def a_landed(i, k):
        spot = xb.at[i, row_block(expert_from(k)), quarter(mine)]
        return remote(spot, spot, a_send.at[i, k], a_recv.at[i, k], (expert_from(k), mine))

    def y_copy(i, dy, k):
        spot = xb.at[i, row_block(expert_from(k)), quarter(mine)]
        return remote(spot, spot, y_send.at[i, dy, k], y_recv.at[i, dy, k], y_peer(dy))

    def c_copy(i, dy, k):
        d = y_from(dy) * CORES + core
        spot = xb.at[i, row_block(expert_from(k)), quarter(d)]
        return remote(spot, spot, c_send.at[i, dy, k], c_recv.at[i, dy, k], sibling)

    def y_landed(i, dy, k):
        d = y_from(dy) * CORES + core
        spot = xb.at[i, row_block(expert_from(k)), quarter(d)]
        return remote(spot, spot, y_send.at[i, dy, k], y_recv.at[i, dy, k], y_peer(dy))

    def c_landed(i, dy, k):
        d = y_from(dy) * CORES + 1 - core
        spot = xb.at[i, row_block(expert_from(k)), quarter(d)]
        return remote(spot, spot, c_send.at[i, dy, k], c_recv.at[i, dy, k], sibling)

    def dispatch(i):
        tok_loads[i].wait()
        sb[i] = jnp.dot(disp[...], tq[i], preferred_element_type=jnp.float32).astype(jnp.bfloat16)

    def keep_own(i):
        xb[i, row_block(me), quarter(mine)] = sb[i, row_block(me), :]

    def send_next(i, k):
        later = k + window

        @pl.when((later < experts) & (k > (0 if i else -1)))
        def _():
            a_copy(i, later).start()

        if i == 0:
            @pl.when(later >= experts)
            def _():
                a_copy(1, later - experts + 1).start()

    def forward(i, k):
        @pl.when(k > 0)
        def _():
            a_landed(i, k).wait_recv()

        send_next(i, k)

        loop(1, ys, lambda dy: y_copy(i, dy, k).start())
        c_copy(i, 0, k).start()

    def second_hop(i, k):
        def one(dy):
            y_landed(i, dy, k).wait_recv()
            c_copy(i, dy, k).start()

        loop(1, ys, one)

    def all_landed(i):
        loop(0, experts, lambda k: loop(0, ys, lambda dy: c_landed(i, dy, k).wait_recv()))

    dispatch(0)
    keep_own(0)
    pl.semaphore_wait(barrier, experts - 1 + ys)
    loop(1, window, lambda k: a_copy(0, k).start())
    dispatch(1)
    keep_own(1)

    disp_t[...] = jnp.transpose(spots).astype(jnp.bfloat16)

    scale = float(ml_dtypes.bfloat16(1.0 / math.sqrt(width)))
    band = 16
    base[...] = (
        iota((band, hidden), 0) * 73856093
        + (iota((band, hidden), 1) + mine * hidden) * 19349663
        + seed[0] * 83492791
    )

    def sign_rows(row0):
        m = base[...] + row0 * 73856093
        m = m ^ (m >> 15)
        m = m * 735632791
        m = m ^ (m >> 13)
        m = m * 1274126177
        m = m ^ (m >> 16)
        signs = jnp.where((m & 32) != 0, scale, -scale).astype(jnp.bfloat16)
        for c in range(chunks):
            w3[pl.ds(pl.multiple_of(row0, band), band), pl.ds((3 * c + 2) * fc, fc)] = (
                signs[:, c * fc:(c + 1) * fc])

    part = width // experts

    def first_steps(k):
        forward(0, k)

        @pl.when(k >= LAG)
        def _():
            second_hop(0, k - LAG)

        loop(0, part // band, lambda j: sign_rows(k * part + j * band))

    loop(0, experts, first_steps)
    loop(experts - LAG, experts, lambda k: second_hop(0, k))
    for load in w_loads[:-1]:
        load.wait()
    all_landed(0)

    def first_dots(c):
        forward(1, c)

        @pl.when(c >= LAG)
        def _():
            second_hop(1, c - LAG)

        first[c] = jnp.dot(
            xb[0], w3[:, pl.ds(pl.multiple_of(c * 3 * fc, 3 * fc), 3 * fc)],
            preferred_element_type=jnp.float32)

    early = min(chunks, experts)
    loop(0, early, first_dots)
    loop(early, experts, lambda k: forward(1, k))
    loop(early - LAG, experts, lambda k: second_hop(1, k))
    w_loads[-1].wait()
    all_landed(1)

    def gates(c, hgrad):
        lanes = [pl.ds(i * fc, fc) for i in range(3)]
        total = jnp.zeros((1, fc), jnp.float32)
        tall = 32
        for row in range(0, rows, tall):
            at = pl.ds(row, tall)
            hg = hgrad[row:row + tall]
            p, up, tangent = (first[c, at, lane] for lane in lanes)
            sig = jax.nn.sigmoid(p)
            slope = sig * (1.0 + p * (1.0 - sig))
            bend = sig * (1.0 - sig) * (2.0 + p * (1.0 - 2.0 * sig))
            both = hg * up
            tg = both * bend * tangent
            parts = (tg, hg * slope * tangent, both * slope)
            for i, value in enumerate(parts):
                h3[at, pl.ds((3 * c + i) * fc, fc)] = value.astype(jnp.bfloat16)
            total += jnp.sum(tangent * tg, axis=0, keepdims=True)
        curv[:, pl.ds(c * fc, fc)] = total

    for c in range(0, chunks, 2):
        n = min(2, chunks - c)
        hgrads = lax.dot_general(
            xb[1], wd[pl.ds(c * fc, n * fc), :], NT, preferred_element_type=jnp.float32)
        for i in range(n):
            gates(c + i, hgrads[:, i * fc:(i + 1) * fc])

    def block_at(d, r):
        index = (lax.div(d, CORES) * rounds + r) * CORES + lax.rem(d, CORES)
        return pl.multiple_of(index * ch, ch)

    def k_copy(dy, r):
        return remote(ksend.at[dy, r], krecv.at[dy, r], k_send.at[dy, r], k_recv.at[dy, r], sibling)

    def p_copy(dy, r):
        return remote(ysend.at[dy, r], yrecv.at[dy, r], p_send.at[dy, r], p_recv.at[dy, r], y_peer(dy))

    def b_copy(r, k):
        e = expert_at(k)
        return remote(fin.at[r, row_block(e), :], ret.at[r, row_block(me), :],
                      b_send.at[r, k], b_recv.at[r, k], (e, mine))

    def b_landed(r, k):
        spot = ret.at[r, row_block(expert_from(k)), :]
        return remote(spot, spot, b_send.at[r, k], b_recv.at[r, k], (expert_from(k), mine))

    def split(step):
        return lax.rem(1 + lax.div(step, rounds), ys), lax.rem(step, rounds)

    def multiply(step):
        dy, r = split(step)
        at = pl.ds(pl.multiple_of((y_at(dy) * rounds + r) * CORES * ch, CORES * ch), CORES * ch)
        pair = lax.dot_general(h3[...], w3[at, :], NT, preferred_element_type=jnp.float32)
        left, right = pair[:, :ch], pair[:, ch:]
        ksend[dy, r] = jnp.where(core == 0, right, left).astype(jnp.bfloat16)
        k_copy(dy, r).start()
        own[dy, r] = jnp.where(core == 0, left, right)

    def finish(step):
        dy, r = split(step)
        k_copy(dy, r).wait_recv()

        @pl.when(dy > 0)
        def _():
            ysend[dy, r] = (own[dy, r] + krecv[dy, r].astype(jnp.float32)).astype(jnp.bfloat16)
            p_copy(dy, r).start()

        @pl.when(dy == 0)
        def _():
            total = own[0, r] + krecv[0, r].astype(jnp.float32)
            for other in range(1, ys):
                p_copy(other, r).wait_recv()
                total += yrecv[other, r].astype(jnp.float32)
            fin[r] = total.astype(jnp.bfloat16)
            loop(1, experts, lambda k: b_copy(r, k).start())
            ret[r, row_block(me), :] = fin[r, row_block(me), :]

    def both_steps(step):
        multiply(step)

        @pl.when(step > 0)
        def _():
            finish(step - 1)

    loop(0, ys * rounds, both_steps)
    finish(ys * rounds - 1)

    def o_spot(d, r):
        return ob.at[:, pl.ds(block_at(d, r), ch)]

    def oy_copy(dy, r):
        spot = o_spot(mine, r)
        return remote(spot, spot, oy_send.at[dy, r], oy_recv.at[dy, r], y_peer(dy))

    def oy_landed(dy, r):
        spot = o_spot(y_from(dy) * CORES + core, r)
        return remote(spot, spot, oy_send.at[dy, r], oy_recv.at[dy, r], y_peer(dy))

    def oc_copy(dy, r):
        spot = o_spot(y_from(dy) * CORES + core, r)
        return remote(spot, spot, oc_send.at[dy, r], oc_recv.at[dy, r], sibling)

    def oc_landed(dy, r):
        spot = o_spot(y_from(dy) * CORES + 1 - core, r)
        return remote(spot, spot, oc_send.at[dy, r], oc_recv.at[dy, r], sibling)

    def combine(r):
        loop(1, experts, lambda k: b_landed(r, k).wait_recv())
        ob[:, pl.ds(block_at(mine, r), ch)] = jnp.dot(
            disp_t[...], ret[r], preferred_element_type=jnp.float32).astype(jnp.bfloat16)
        loop(1, ys, lambda dy: oy_copy(dy, r).start())
        oc_copy(0, r).start()

    loop(0, rounds, combine)

    def out_hop(r):
        def one(dy):
            oy_landed(dy, r).wait_recv()
            oc_copy(dy, r).start()

        loop(1, ys, one)

    loop(0, rounds, out_hop)
    loop(0, rounds, lambda r: loop(0, ys, lambda dy: oc_landed(dy, r).wait_recv()))
    write = pltpu.make_async_copy(ob, out_hbm, out_sem)
    write.start()

    def drain(i):
        def one(k):
            @pl.when(k > 0)
            def _():
                a_copy(i, k).wait_send()

            loop(1, ys, lambda dy: y_copy(i, dy, k).wait_send())
            loop(0, ys, lambda dy: c_copy(i, dy, k).wait_send())

        loop(0, experts, one)

    loop(0, 2, drain)

    def drain_out(r):
        loop(0, ys, lambda dy: k_copy(dy, r).wait_send())
        loop(1, ys, lambda dy: p_copy(dy, r).wait_send())
        loop(1, experts, lambda k: b_copy(r, k).wait_send())
        loop(1, ys, lambda dy: oy_copy(dy, r).wait_send())
        loop(0, ys, lambda dy: oc_copy(dy, r).wait_send())

    loop(0, rounds, drain_out)
    write.wait()


def body(tokens, cotangent, expert_route, w_gate, w_up, w_down, sign_seeds):
    experts = lax.axis_size("expert")
    dps = lax.axis_size("dp")
    toks, width = tokens.shape
    hidden = w_gate.shape[2]
    slots = max(2, 2 * toks // experts)
    rows = experts * slots
    ys = dps // CORES
    qw = width // dps
    ch = min(256, qw)
    rounds = qw // ch
    fc = 256 if hidden % 256 == 0 else 128
    chunks = hidden // fc
    cfg = (experts, dps, toks, width, hidden, slots, fc, qw, ch)
    bf, f32 = jnp.bfloat16, jnp.float32
    vm, dma = pltpu.VMEM, pltpu.SemaphoreType.DMA
    anywhere = pl.BlockSpec(memory_space=pl.ANY)
    in_vmem = pl.BlockSpec(memory_space=pltpu.VMEM)
    return pl.pallas_call(
        functools.partial(kernel, cfg),
        out_shape=(
            jax.ShapeDtypeStruct((toks, width), bf),
            jax.ShapeDtypeStruct((1, hidden), f32),
        ),
        in_specs=[in_vmem, pl.BlockSpec(memory_space=pltpu.SMEM)] + [anywhere] * 5,
        out_specs=(anywhere, in_vmem),
        scratch_shapes=[
            vm((width, 3 * hidden), bf), vm((hidden, width), bf), vm((16, hidden), jnp.int32),
            vm((rows, toks), bf), vm((toks, rows), bf),
            vm((2, toks, qw), bf), vm((2, rows, qw), bf), vm((2, rows, width), bf),
            vm((chunks, rows, 3 * fc), f32), vm((rows, 3 * hidden), bf),
            vm((ys, rounds, rows, ch), bf), vm((ys, rounds, rows, ch), bf),
            vm((ys, rounds, rows, ch), f32),
            vm((ys, rounds, rows, ch), bf), vm((ys, rounds, rows, ch), bf),
            vm((rounds, rows, ch), bf), vm((rounds, rows, ch), bf),
            vm((toks, width), bf),
            dma((3, chunks)), dma((2,)), dma,
            dma((2, experts)), dma((2, experts)),
            dma((2, ys, experts)), dma((2, ys, experts)),
            dma((2, ys, experts)), dma((2, ys, experts)),
            dma((ys, rounds)), dma((ys, rounds)),
            dma((ys, rounds)), dma((ys, rounds)),
            dma((rounds, experts)), dma((rounds, experts)),
            dma((ys, rounds)), dma((ys, rounds)),
            dma((ys, rounds)), dma((ys, rounds)),
        ],
        compiler_params=pltpu.CompilerParams(
            collective_id=0, has_side_effects=True, vmem_limit_bytes=63 * 1024 * 1024
        ),
    )(
        expert_route.reshape(1, toks), sign_seeds,
        tokens, cotangent, w_gate, w_up, w_down,
    )


def solution(mesh):
    in_specs = (
        P("expert", None),
        P("expert", None),
        P("expert", None),
        P("expert", None, "dp"),
        P("expert", None, "dp"),
        P("expert", "dp", None),
        P("expert"),
    )
    out_specs = (P("expert", None), P("expert", "dp"))
    return jax.shard_map(body, mesh=mesh, in_specs=in_specs, out_specs=out_specs, check_vma=False)
```

```python
import functools
import math

import jax
import jax.numpy as jnp
import ml_dtypes
from jax import lax
from jax.experimental import pallas as pl
from jax.experimental.pallas import tpu as pltpu
from jax.sharding import PartitionSpec as P

MESH = pl.DeviceIdType.MESH
CORES = 2
LAG = 2
WINDOW = 3
NT = (((1,), (1,)), ((), ()))


def loop(low, high, fn):
    def step(index, carry):
        fn(index)
        return carry

    lax.fori_loop(low, high, step, 0)


def kernel(
    cfg,
    route_row, seed, tok, cot, wg_hbm, wu_hbm, wd_hbm,
    out_hbm, curv,
    w3, wd, base, disp, disp_t, tq, sb, xb, first, h3,
    ksend, krecv, own, ysend, yrecv, fin, ret, ob,
    w_sem, t_sem, out_sem, a_send, a_recv, y_send, y_recv, c_send, c_recv,
    k_send, k_recv, p_send, p_recv, b_send, b_recv, oy_send, oy_recv, oc_send, oc_recv,
):
    experts, dps, toks, width, hidden, slots, fc, qw, ch = cfg
    ys = dps // CORES
    rounds = qw // ch
    chunks = hidden // fc
    rows = experts * slots
    window = min(WINDOW, experts - 1)
    me = lax.axis_index("expert")
    mine = lax.axis_index("dp")
    core = lax.rem(mine, CORES)
    y = lax.div(mine, CORES)
    sibling = (me, y * CORES + 1 - core)

    def expert_at(k):
        return lax.rem(me + k, experts)

    def expert_from(k):
        return lax.rem(me - k + experts, experts)

    def y_at(dy):
        return lax.rem(y + dy, ys)

    def y_from(dy):
        return lax.rem(y - dy + ys, ys)

    def y_peer(dy):
        return (me, y_at(dy) * CORES + core)

    def row_block(e):
        return pl.ds(pl.multiple_of(e * slots, slots), slots)

    def quarter(d):
        return pl.ds(pl.multiple_of(d * qw, qw), qw)

    def remote(src, dst, s, r, dev):
        return pltpu.make_async_remote_copy(
            src_ref=src, dst_ref=dst, send_sem=s, recv_sem=r, device_id=dev, device_id_type=MESH
        )

    tok_loads = [
        pltpu.make_async_copy(ref.at[:, quarter(mine)], tq.at[i], t_sem.at[i])
        for i, ref in enumerate((tok, cot))
    ]
    for load in tok_loads:
        load.start()
    w_loads = [
        pltpu.make_async_copy(
            src.at[0, :, pl.ds(c * fc, fc)], w3.at[:, pl.ds((3 * c + i) * fc, fc)], w_sem.at[i, c]
        )
        for c in range(chunks)
        for i, src in enumerate((wg_hbm, wu_hbm))
    ]
    w_loads.append(pltpu.make_async_copy(wd_hbm.at[0], wd, w_sem.at[2, 0]))
    for load in w_loads:
        load.start()

    barrier = pltpu.get_barrier_semaphore()
    loop(1, experts, lambda k: pl.semaphore_signal(
        barrier, inc=1, device_id=(expert_at(k), mine), device_id_type=MESH))
    loop(1, ys, lambda dy: pl.semaphore_signal(
        barrier, inc=1, device_id=y_peer(dy), device_id_type=MESH))
    pl.semaphore_signal(barrier, inc=1, device_id=sibling, device_id_type=MESH)

    def iota(shape, dim):
        return lax.broadcasted_iota(jnp.int32, shape, dim)

    def ones_where(cond):
        return jnp.where(cond, 1.0, 0.0).astype(jnp.float32)

    pad = max(16, experts)
    hot = ones_where(iota((pad, toks), 0) == route_row[...])
    upper = ones_where(iota((toks, toks), 0) <= iota((toks, toks), 1)).astype(jnp.bfloat16)
    seen = jnp.dot(hot.astype(jnp.bfloat16), upper, preferred_element_type=jnp.float32)
    place = jnp.sum(seen * hot, axis=0, keepdims=True) - 1.0
    target = route_row[...] * slots + place.astype(jnp.int32)
    spots = ones_where(iota((rows, toks), 0) == target)
    disp[...] = spots.astype(jnp.bfloat16)

    def a_copy(i, k):
        e = expert_at(k)
        return remote(sb.at[i, row_block(e), :], xb.at[i, row_block(me), quarter(mine)],
                      a_send.at[i, k], a_recv.at[i, k], (e, mine))

    def a_landed(i, k):
        spot = xb.at[i, row_block(expert_from(k)), quarter(mine)]
        return remote(spot, spot, a_send.at[i, k], a_recv.at[i, k], (expert_from(k), mine))

    def y_copy(i, dy, k):
        spot = xb.at[i, row_block(expert_from(k)), quarter(mine)]
        return remote(spot, spot, y_send.at[i, dy, k], y_recv.at[i, dy, k], y_peer(dy))

    def c_copy(i, dy, k):
        d = y_from(dy) * CORES + core
        spot = xb.at[i, row_block(expert_from(k)), quarter(d)]
        return remote(spot, spot, c_send.at[i, dy, k], c_recv.at[i, dy, k], sibling)

    def y_landed(i, dy, k):
        d = y_from(dy) * CORES + core
        spot = xb.at[i, row_block(expert_from(k)), quarter(d)]
        return remote(spot, spot, y_send.at[i, dy, k], y_recv.at[i, dy, k], y_peer(dy))

    def c_landed(i, dy, k):
        d = y_from(dy) * CORES + 1 - core
        spot = xb.at[i, row_block(expert_from(k)), quarter(d)]
        return remote(spot, spot, c_send.at[i, dy, k], c_recv.at[i, dy, k], sibling)

    def dispatch(i):
        tok_loads[i].wait()
        sb[i] = jnp.dot(disp[...], tq[i], preferred_element_type=jnp.float32).astype(jnp.bfloat16)

    def keep_own(i):
        xb[i, row_block(me), quarter(mine)] = sb[i, row_block(me), :]

    def send_next(i, k):
        later = k + window

        @pl.when((later < experts) & (k > (0 if i else -1)))
        def _():
            a_copy(i, later).start()

        if i == 0:
            @pl.when(later >= experts)
            def _():
                a_copy(1, later - experts + 1).start()

    def forward(i, k):
        @pl.when(k > 0)
        def _():
            a_landed(i, k).wait_recv()

        send_next(i, k)

        loop(1, ys, lambda dy: y_copy(i, dy, k).start())
        c_copy(i, 0, k).start()

    def second_hop(i, k):
        def one(dy):
            y_landed(i, dy, k).wait_recv()
            c_copy(i, dy, k).start()

        loop(1, ys, one)

    def all_landed(i):
        loop(0, experts, lambda k: loop(0, ys, lambda dy: c_landed(i, dy, k).wait_recv()))

    dispatch(0)
    keep_own(0)
    pl.semaphore_wait(barrier, experts - 1 + ys)
    loop(1, window, lambda k: a_copy(0, k).start())
    dispatch(1)
    keep_own(1)

    disp_t[...] = jnp.transpose(spots).astype(jnp.bfloat16)

    scale = float(ml_dtypes.bfloat16(1.0 / math.sqrt(width)))
    band = 16
    base[...] = (
        iota((band, hidden), 0) * 73856093
        + (iota((band, hidden), 1) + mine * hidden) * 19349663
        + seed[0] * 83492791
    )

    def sign_rows(row0):
        m = base[...] + row0 * 73856093
        m = m ^ (m >> 15)
        m = m * 735632791
        m = m ^ (m >> 13)
        m = m * 1274126177
        m = m ^ (m >> 16)
        signs = jnp.where((m & 32) != 0, scale, -scale).astype(jnp.bfloat16)
        for c in range(chunks):
            w3[pl.ds(pl.multiple_of(row0, band), band), pl.ds((3 * c + 2) * fc, fc)] = (
                signs[:, c * fc:(c + 1) * fc])

    part = width // experts

    def first_steps(k):
        forward(0, k)

        @pl.when(k >= LAG)
        def _():
            second_hop(0, k - LAG)

        loop(0, part // band, lambda j: sign_rows(k * part + j * band))

    loop(0, experts, first_steps)
    loop(experts - LAG, experts, lambda k: second_hop(0, k))
    for load in w_loads[:-1]:
        load.wait()
    all_landed(0)

    def first_dots(c):
        forward(1, c)

        @pl.when(c >= LAG)
        def _():
            second_hop(1, c - LAG)

        first[c] = jnp.dot(
            xb[0], w3[:, pl.ds(pl.multiple_of(c * 3 * fc, 3 * fc), 3 * fc)],
            preferred_element_type=jnp.float32)

    early = min(chunks, experts)
    loop(0, early, first_dots)
    loop(early, experts, lambda k: forward(1, k))
    loop(early - LAG, experts, lambda k: second_hop(1, k))
    w_loads[-1].wait()
    all_landed(1)

    def gates(c, hgrad):
        lanes = [pl.ds(i * fc, fc) for i in range(3)]
        total = jnp.zeros((1, fc), jnp.float32)
        tall = 32
        for row in range(0, rows, tall):
            at = pl.ds(row, tall)
            hg = hgrad[row:row + tall]
            p, up, tangent = (first[c, at, lane] for lane in lanes)
            sig = jax.nn.sigmoid(p)
            slope = sig * (1.0 + p * (1.0 - sig))
            bend = sig * (1.0 - sig) * (2.0 + p * (1.0 - 2.0 * sig))
            both = hg * up
            tg = both * bend * tangent
            parts = (tg, hg * slope * tangent, both * slope)
            for i, value in enumerate(parts):
                h3[at, pl.ds((3 * c + i) * fc, fc)] = value.astype(jnp.bfloat16)
            total += jnp.sum(tangent * tg, axis=0, keepdims=True)
        curv[:, pl.ds(c * fc, fc)] = total

    for c in range(0, chunks, 2):
        n = min(2, chunks - c)
        hgrads = lax.dot_general(
            xb[1], wd[pl.ds(c * fc, n * fc), :], NT, preferred_element_type=jnp.float32)
        for i in range(n):
            gates(c + i, hgrads[:, i * fc:(i + 1) * fc])

    def block_at(d, r):
        index = (lax.div(d, CORES) * rounds + r) * CORES + lax.rem(d, CORES)
        return pl.multiple_of(index * ch, ch)

    def k_copy(dy, r):
        return remote(ksend.at[dy, r], krecv.at[dy, r], k_send.at[dy, r], k_recv.at[dy, r], sibling)

    def p_copy(dy, r):
        return remote(ysend.at[dy, r], yrecv.at[dy, r], p_send.at[dy, r], p_recv.at[dy, r], y_peer(dy))

    def b_copy(r, k):
        e = expert_at(k)
        return remote(fin.at[r, row_block(e), :], ret.at[r, row_block(me), :],
                      b_send.at[r, k], b_recv.at[r, k], (e, mine))

    def b_landed(r, k):
        spot = ret.at[r, row_block(expert_from(k)), :]
        return remote(spot, spot, b_send.at[r, k], b_recv.at[r, k], (expert_from(k), mine))

    def split(step):
        return lax.rem(1 + lax.div(step, rounds), ys), lax.rem(step, rounds)

    def multiply(step):
        dy, r = split(step)
        at = pl.ds(pl.multiple_of((y_at(dy) * rounds + r) * CORES * ch, CORES * ch), CORES * ch)
        pair = lax.dot_general(h3[...], w3[at, :], NT, preferred_element_type=jnp.float32)
        left, right = pair[:, :ch], pair[:, ch:]
        ksend[dy, r] = jnp.where(core == 0, right, left).astype(jnp.bfloat16)
        k_copy(dy, r).start()
        own[dy, r] = jnp.where(core == 0, left, right)

    def finish(step):
        dy, r = split(step)
        k_copy(dy, r).wait_recv()

        @pl.when(dy > 0)
        def _():
            ysend[dy, r] = (own[dy, r] + krecv[dy, r].astype(jnp.float32)).astype(jnp.bfloat16)
            p_copy(dy, r).start()

        @pl.when(dy == 0)
        def _():
            total = own[0, r] + krecv[0, r].astype(jnp.float32)
            for other in range(1, ys):
                p_copy(other, r).wait_recv()
                total += yrecv[other, r].astype(jnp.float32)
            fin[r] = total.astype(jnp.bfloat16)
            loop(1, experts, lambda k: b_copy(r, k).start())
            ret[r, row_block(me), :] = fin[r, row_block(me), :]

    def both_steps(step):
        multiply(step)

        @pl.when(step > 0)
        def _():
            finish(step - 1)

    loop(0, ys * rounds, both_steps)
    finish(ys * rounds - 1)

    def o_spot(d, r):
        return ob.at[:, pl.ds(block_at(d, r), ch)]

    def oy_copy(dy, r):
        spot = o_spot(mine, r)
        return remote(spot, spot, oy_send.at[dy, r], oy_recv.at[dy, r], y_peer(dy))

    def oy_landed(dy, r):
        spot = o_spot(y_from(dy) * CORES + core, r)
        return remote(spot, spot, oy_send.at[dy, r], oy_recv.at[dy, r], y_peer(dy))

    def oc_copy(dy, r):
        spot = o_spot(y_from(dy) * CORES + core, r)
        return remote(spot, spot, oc_send.at[dy, r], oc_recv.at[dy, r], sibling)

    def oc_landed(dy, r):
        spot = o_spot(y_from(dy) * CORES + 1 - core, r)
        return remote(spot, spot, oc_send.at[dy, r], oc_recv.at[dy, r], sibling)

    def combine(r):
        loop(1, experts, lambda k: b_landed(r, k).wait_recv())
        ob[:, pl.ds(block_at(mine, r), ch)] = jnp.dot(
            disp_t[...], ret[r], preferred_element_type=jnp.float32).astype(jnp.bfloat16)
        loop(1, ys, lambda dy: oy_copy(dy, r).start())
        oc_copy(0, r).start()

    loop(0, rounds, combine)

    def out_hop(r):
        def one(dy):
            oy_landed(dy, r).wait_recv()
            oc_copy(dy, r).start()

        loop(1, ys, one)

    loop(0, rounds, out_hop)
    loop(0, rounds, lambda r: loop(0, ys, lambda dy: oc_landed(dy, r).wait_recv()))
    write = pltpu.make_async_copy(ob, out_hbm, out_sem)
    write.start()

    def drain(i):
        def one(k):
            @pl.when(k > 0)
            def _():
                a_copy(i, k).wait_send()

            loop(1, ys, lambda dy: y_copy(i, dy, k).wait_send())
            loop(0, ys, lambda dy: c_copy(i, dy, k).wait_send())

        loop(0, experts, one)

    loop(0, 2, drain)

    def drain_out(r):
        loop(0, ys, lambda dy: k_copy(dy, r).wait_send())
        loop(1, ys, lambda dy: p_copy(dy, r).wait_send())
        loop(1, experts, lambda k: b_copy(r, k).wait_send())
        loop(1, ys, lambda dy: oy_copy(dy, r).wait_send())
        loop(0, ys, lambda dy: oc_copy(dy, r).wait_send())

    loop(0, rounds, drain_out)
    write.wait()


def body(tokens, cotangent, expert_route, w_gate, w_up, w_down, sign_seeds):
    experts = lax.axis_size("expert")
    dps = lax.axis_size("dp")
    toks, width = tokens.shape
    hidden = w_gate.shape[2]
    slots = max(2, 2 * toks // experts)
    rows = experts * slots
    ys = dps // CORES
    qw = width // dps
    ch = min(128, qw)
    rounds = qw // ch
    fc = 256 if hidden % 256 == 0 else 128
    chunks = hidden // fc
    cfg = (experts, dps, toks, width, hidden, slots, fc, qw, ch)
    bf, f32 = jnp.bfloat16, jnp.float32
    vm, dma = pltpu.VMEM, pltpu.SemaphoreType.DMA
    anywhere = pl.BlockSpec(memory_space=pl.ANY)
    in_vmem = pl.BlockSpec(memory_space=pltpu.VMEM)
    return pl.pallas_call(
        functools.partial(kernel, cfg),
        out_shape=(
            jax.ShapeDtypeStruct((toks, width), bf),
            jax.ShapeDtypeStruct((1, hidden), f32),
        ),
        in_specs=[in_vmem, pl.BlockSpec(memory_space=pltpu.SMEM)] + [anywhere] * 5,
        out_specs=(anywhere, in_vmem),
        scratch_shapes=[
            vm((width, 3 * hidden), bf), vm((hidden, width), bf), vm((16, hidden), jnp.int32),
            vm((rows, toks), bf), vm((toks, rows), bf),
            vm((2, toks, qw), bf), vm((2, rows, qw), bf), vm((2, rows, width), bf),
            vm((chunks, rows, 3 * fc), f32), vm((rows, 3 * hidden), bf),
            vm((ys, rounds, rows, ch), bf), vm((ys, rounds, rows, ch), bf),
            vm((ys, rounds, rows, ch), f32),
            vm((ys, rounds, rows, ch), bf), vm((ys, rounds, rows, ch), bf),
            vm((rounds, rows, ch), bf), vm((rounds, rows, ch), bf),
            vm((toks, width), bf),
            dma((3, chunks)), dma((2,)), dma,
            dma((2, experts)), dma((2, experts)),
            dma((2, ys, experts)), dma((2, ys, experts)),
            dma((2, ys, experts)), dma((2, ys, experts)),
            dma((ys, rounds)), dma((ys, rounds)),
            dma((ys, rounds)), dma((ys, rounds)),
            dma((rounds, experts)), dma((rounds, experts)),
            dma((ys, rounds)), dma((ys, rounds)),
            dma((ys, rounds)), dma((ys, rounds)),
        ],
        compiler_params=pltpu.CompilerParams(
            collective_id=0, has_side_effects=True, vmem_limit_bytes=63 * 1024 * 1024
        ),
    )(
        expert_route.reshape(1, toks), sign_seeds,
        tokens, cotangent, w_gate, w_up, w_down,
    )


def solution(mesh):
    in_specs = (
        P("expert", None),
        P("expert", None),
        P("expert", None),
        P("expert", None, "dp"),
        P("expert", None, "dp"),
        P("expert", "dp", None),
        P("expert"),
    )
    out_specs = (P("expert", None), P("expert", "dp"))
    return jax.shard_map(body, mesh=mesh, in_specs=in_specs, out_specs=out_specs, check_vma=False)
```
